32 devices in a mesh: groups: 2 (over x), train: 8 (over z, y), query: 2 (over core).
Axes of the slice: x: 2, y: 2, z: 4, core: 2. Of those that a mesh axis runs over, the one named last changes fastest.
Arguments:
- train_grads: float32 [8192, 1024], P(('groups', 'train', 'query')), parts along dimension 0, may hold values from -60 to 60, as said below
- query_grads: float32 [2048, 1024], P(('groups', 'query'), 'train'), parts along dimension 0, may hold values from -6 to 6
Outputs:
- scores: float32 [2048, 4096], P(('groups', 'query'), 'train'), parts along dimension 0
The draws below stay inside these ranges and needn't reach their ends.
There are 2 independent parts, one for each index of `groups`. The reference program is written for one: setup_inputs(seed, part) draws one part's arguments, and reference() takes and returns one part's arrays. A program takes and returns all parts, laid end to end along the dimension named above; each array names one. Nothing has to cross between parts.
Inputs may be any that keep to these rules, and one draw needn't show every extreme that they name: `train_grads`: each entry is a sum of terms of varied size, times a document scale and a coordinate scale.
All inputs are finite; a program needn't handle non-finite values.
Results may differ from the reference program's by a relative error of at most 0.0003.
Values sent between devices are 32-bit elements; how exact they have to be, the bound alone decides.
A program may use at most 128 MiB of HBM per device.

```python
import math
import jax
import jax.numpy as jnp
from jax import lax

K = 1024
TRAIN = 4096
QUERIES = 1024


def shared_terms(key_signs, key_levels, key_counts, key_value):
    topics = K // 2
    signs = (2 * jax.random.randint(key_signs, (topics, K), 0, 2) - 1).astype(jnp.float32)
    levels = jax.random.randint(key_levels, (topics,), 0, 88)
    magnitude_table = jnp.asarray([1, 2, 3, 4, 6, 8, 11, 15], jnp.int32)
    power_table = jnp.asarray([2.0 ** (-step) for step in range(11)], jnp.float32)
    magnitudes = magnitude_table[levels % 8]
    powers = power_table[levels // 8]
    raw = jax.random.randint(key_counts, (TRAIN, topics), 0, 1048576)
    counts = raw % (2 * magnitudes[None, :] + 1) - magnitudes[None, :]
    weights = counts.astype(jnp.float32) * powers[None, :]
    mixed = jnp.dot(weights, signs, preferred_element_type=jnp.float32, precision=lax.Precision.HIGHEST)
    return mixed * key_value


def draw_train_grads(key, part):
    key = jax.random.fold_in(key, 7)
    first = jax.random.fold_in(key, 0)
    second = jax.random.fold_in(key, 1)
    third = jax.random.fold_in(key, 2)
    fifth = jax.random.fold_in(key, 4)
    sixth = jax.random.fold_in(key, 5)
    seventh = jax.random.fold_in(key, 6)
    mixed = shared_terms(fifth, sixth, seventh, math.sqrt(75.0 / K))
    base = jnp.clip(jax.random.normal(first, (TRAIN, K), jnp.float32), -6.0, 6.0)
    row_scale = jnp.exp(jax.random.uniform(second, (TRAIN, 1), jnp.float32, 0.0, math.log(10.0))) / 3.0
    col_scale = jnp.exp(jax.random.uniform(third, (1, K), jnp.float32, math.log(0.3), math.log(3.0)))
    values = (base + mixed) * 0.1 * row_scale * col_scale
    return jnp.clip(values, -60.0, 60.0)


def block_scale(rng, shape, shards, low, largest):
    level = 1.0
    for position, parts in shards:
        draws = jax.random.uniform(jax.random.fold_in(jax.random.fold_in(rng, 6), position), (parts,), jnp.float32, low / len(shards), largest / len(shards))
        level = level * jnp.repeat(jnp.exp(draws), shape[position] // parts).reshape((-1,) + (1,) * (len(shape) - 1 - position))
    return level


def centred(stream_key, extent, width, reach, cuts=(), held_as=jnp.bfloat16):
    array = width * jax.random.normal(stream_key, extent, jnp.float32)
    if cuts:
        array = array * block_scale(stream_key, extent, cuts, -0.22, 0.18)
    return jnp.clip(array, -reach, reach).astype(held_as)


def setup_inputs(seed: int = 0, part: int = 0) -> dict:
    key_of = jax.random.split(jax.random.key(seed), 3)
    part_keys = jax.random.split(jax.random.fold_in(key_of[2], part), 3)
    return {
        "train_grads": draw_train_grads(jax.random.fold_in(jax.random.fold_in(key_of[2], part), 71), part),
        "query_grads": centred(part_keys[1], (QUERIES, K), 1.0, 6.0, ((0, 2), (1, 8)), jnp.float32),
    }


def solve_rows(lower, queries):
    middle = lax.linalg.triangular_solve(lower, queries, left_side=False, lower=True, transpose_a=True)
    return lax.linalg.triangular_solve(lower, middle, left_side=False, lower=True, transpose_a=False)

def reference(train_grads, query_grads):
    gram = jnp.dot(train_grads.T.astype(jnp.float32), train_grads.astype(jnp.float32), preferred_element_type=jnp.float32, precision=lax.Precision.HIGHEST)
    shift = 0.1 * jnp.trace(gram) / (TRAIN * K)
    curvature = gram / TRAIN + shift * jnp.eye(K, dtype=jnp.float32)
    lower = jnp.linalg.cholesky(curvature)
    precond = solve_rows(lower, query_grads)
    scores = jnp.dot(precond.astype(jnp.float32), train_grads.T.astype(jnp.float32), preferred_element_type=jnp.float32, precision=lax.Precision.HIGHEST)
    return scores / jnp.sqrt(jnp.float32(K))
```

```python
import functools

import jax
import jax.numpy as jnp
from jax import lax
from jax.experimental import pallas as pl
from jax.experimental.pallas import tpu as pltpu
from jax.sharding import PartitionSpec as P

HIGHEST = lax.Precision.HIGHEST
SIDE = 128
ROWS = 8


def dot(a, b, dims=((1,), (0,))):
    return lax.dot_general(
        a, b, (dims, ((), ())), precision=HIGHEST, preferred_element_type=jnp.float32
    )


def invert_small(cols, row):
    for s in range(ROWS):
        inv = 1.0 / jnp.broadcast_to(cols[s][s : s + 1], cols[s].shape)
        here = row == s
        pivot = cols[s]
        out = []
        for j in range(ROWS):
            if j == s:
                out.append(jnp.where(here, inv, -pivot * inv))
            else:
                r = jnp.broadcast_to(cols[j][s : s + 1], pivot.shape) * inv
                out.append(jnp.where(here, r, cols[j] - pivot * r))
        cols = out
    return cols


def spread(block, lane):
    return jnp.take_along_axis(block, jnp.full(block.shape, lane, jnp.int32), axis=1)


def invert_block(d_ref):
    panels = SIDE // ROWS
    row = lax.broadcasted_iota(jnp.int32, (ROWS, SIDE), 0)
    lane = lax.broadcasted_iota(jnp.int32, (ROWS, SIDE), 1)

    def step(g, carry):
        base = g * ROWS
        at = pl.ds(pl.multiple_of(base, ROWS), ROWS)
        own = d_ref[at, :]
        cols = invert_small([spread(own, base + s) for s in range(ROWS)], row)
        inside = (lane >= base) & (lane < base + ROWS)
        start = jnp.where(inside, jnp.where(lane - base == row, 1.0, 0.0), own)
        fresh = cols[0] * jnp.broadcast_to(start[0:1], start.shape)
        for s in range(1, ROWS):
            fresh = fresh + cols[s] * jnp.broadcast_to(start[s : s + 1], start.shape)
        wide = [jnp.broadcast_to(fresh[s : s + 1], fresh.shape) for s in range(ROWS)]
        for i in range(panels):
            block = d_ref[i * ROWS : (i + 1) * ROWS, :]
            new = jnp.where(inside, 0.0, block)
            for s in range(ROWS):
                new = new - spread(block, base + s) * wide[s]
            d_ref[i * ROWS : (i + 1) * ROWS, :] = new
        d_ref[at, :] = fresh
        return carry

    lax.fori_loop(0, panels, step, 0)


def solve_kernel(gram_ref, query_ref, out_ref, a_ref, inv_ref):
    width = gram_ref.shape[0]
    count = width // SIDE
    eye = lax.broadcasted_iota(jnp.int32, (SIDE, SIDE), 0) == lax.broadcasted_iota(
        jnp.int32, (SIDE, SIDE), 1
    )
    span = [slice(k * SIDE, (k + 1) * SIDE) for k in range(count)]
    diag = jnp.zeros((SIDE, SIDE), jnp.float32)
    for k in range(count):
        diag = diag + jnp.where(eye, gram_ref[span[k], span[k]], 0.0)
    shift = 0.1 * jnp.sum(diag) / width
    for k in range(count):
        a_ref[span[k], k * SIDE :] = gram_ref[span[k], k * SIDE :]
        a_ref[span[k], span[k]] += jnp.where(eye, shift, 0.0)
    out_ref[...] = query_ref[...]
    for k in range(count):
        inv_ref[k] = a_ref[span[k], span[k]]
        invert_block(inv_ref.at[k])
        if k + 1 == count:
            break
        rest = a_ref[span[k], (k + 1) * SIDE :]
        w = dot(inv_ref[k], rest)
        for i in range(k + 1, count):
            off = (i - k - 1) * SIDE
            a_ref[span[i], i * SIDE :] -= dot(
                rest[:, off : off + SIDE], w[:, off:], ((0,), (0,))
            )
        a_ref[span[k], (k + 1) * SIDE :] = w
        out_ref[:, (k + 1) * SIDE :] -= dot(out_ref[:, span[k]], w)
    for k in reversed(range(count)):
        z = dot(out_ref[:, span[k]], inv_ref[k])
        if k + 1 < count:
            z = z - dot(
                out_ref[:, (k + 1) * SIDE :], a_ref[span[k], (k + 1) * SIDE :], ((1,), (1,))
            )
        out_ref[:, span[k]] = z


def solve_rows(gram, queries):
    width = gram.shape[0]
    vmem = pl.BlockSpec(memory_space=pltpu.VMEM)
    return pl.pallas_call(
        solve_kernel,
        out_shape=jax.ShapeDtypeStruct(queries.shape, jnp.float32),
        in_specs=[vmem, vmem],
        out_specs=vmem,
        scratch_shapes=[
            pltpu.VMEM((width, width), jnp.float32),
            pltpu.VMEM((width // SIDE, SIDE, SIDE), jnp.float32),
        ],
        compiler_params=pltpu.CompilerParams(vmem_limit_bytes=48 * 2**20),
    )(gram, queries)


def shards(train_grads, query_grads):
    width = train_grads.shape[1]
    half = width // lax.axis_size("query")
    stacked = lax.all_gather(train_grads, "query", axis=0, tiled=True)
    own_cols = lax.dynamic_slice_in_dim(stacked, lax.axis_index("query") * half, half, 1)
    share = lax.psum_scatter(
        jnp.dot(stacked.T, own_cols, preferred_element_type=jnp.float32, precision=HIGHEST),
        "train",
        scatter_dimension=0,
        tiled=True,
    )
    tall = lax.all_gather(share, "train", axis=0, tiled=True)
    gram = lax.all_gather(tall, "query", axis=1, tiled=True)
    count_docs = lax.axis_size("train") * lax.axis_size("query") * train_grads.shape[0]
    queries = lax.all_gather(query_grads, "train", axis=1, tiled=True)
    precond = solve_rows(gram, queries)
    scores = jnp.dot(precond, stacked.T, preferred_element_type=jnp.float32, precision=HIGHEST)
    return scores * (count_docs / jnp.sqrt(jnp.float32(width)))


def solution(mesh):
    in_specs = (P(("groups", "train", "query"), None), P(("groups", "query"), "train"))
    out_specs = P(("groups", "query"), "train")
    return jax.shard_map(shards, mesh=mesh, in_specs=in_specs, out_specs=out_specs, check_vma=False)
```

```python
import functools

import jax
import jax.numpy as jnp
from jax import lax
from jax.experimental import pallas as pl
from jax.experimental.pallas import tpu as pltpu
from jax.sharding import PartitionSpec as P

HIGHEST = lax.Precision.HIGHEST
SIDE = 128
ROWS = 8


def dot(a, b, dims=((1,), (0,))):
    return lax.dot_general(
        a, b, (dims, ((), ())), precision=HIGHEST, preferred_element_type=jnp.float32
    )


def invert_small(cols, row):
    for s in range(ROWS):
        inv = 1.0 / jnp.broadcast_to(cols[s][s : s + 1], cols[s].shape)
        here = row == s
        pivot = cols[s]
        out = []
        for j in range(ROWS):
            if j == s:
                out.append(jnp.where(here, inv, -pivot * inv))
            else:
                r = jnp.broadcast_to(cols[j][s : s + 1], pivot.shape) * inv
                out.append(jnp.where(here, r, cols[j] - pivot * r))
        cols = out
    return cols


def spread(block, lane):
    return jnp.take_along_axis(block, jnp.full(block.shape, lane, jnp.int32), axis=1)


def invert_block(d_ref):
    panels = SIDE // ROWS
    row = lax.broadcasted_iota(jnp.int32, (ROWS, SIDE), 0)
    lane = lax.broadcasted_iota(jnp.int32, (ROWS, SIDE), 1)

    def step(g, carry):
        base = g * ROWS
        at = pl.ds(pl.multiple_of(base, ROWS), ROWS)
        own = d_ref[at, :]
        cols = invert_small([spread(own, base + s) for s in range(ROWS)], row)
        inside = (lane >= base) & (lane < base + ROWS)
        start = jnp.where(inside, jnp.where(lane - base == row, 1.0, 0.0), own)
        fresh = cols[0] * jnp.broadcast_to(start[0:1], start.shape)
        for s in range(1, ROWS):
            fresh = fresh + cols[s] * jnp.broadcast_to(start[s : s + 1], start.shape)
        wide = [jnp.broadcast_to(fresh[s : s + 1], fresh.shape) for s in range(ROWS)]
        for i in range(panels):
            block = d_ref[i * ROWS : (i + 1) * ROWS, :]
            new = jnp.where(inside, 0.0, block)
            for s in range(ROWS):
                new = new - spread(block, base + s) * wide[s]
            d_ref[i * ROWS : (i + 1) * ROWS, :] = new
        d_ref[at, :] = fresh
        return carry

    lax.fori_loop(0, panels, step, 0)


def band_width(width):
    return width // 2 + SIDE


def gram_kernel(teams, own_ref, stacked_ref, band_ref, turned, part, slots, sems, pair_sem):
    docs, width = own_ref.shape
    half, wide = width // 2, band_width(width)
    rows = half // teams
    t, c = lax.axis_index("train"), lax.axis_index("query")
    other = 1 - c

    def mine(team, core):
        return pl.ds(pl.multiple_of(core * half + team * rows, rows), rows)

    def away(d):
        return lax.rem(t + d, teams), lax.rem(t + teams - d, teams)

    def push(src, dst, send, recv, team, core):
        return pltpu.make_async_remote_copy(
            src_ref=src,
            dst_ref=dst,
            send_sem=send,
            recv_sem=recv,
            device_id={"train": team, "query": core},
            device_id_type=pl.DeviceIdType.MESH,
        )

    barrier = pltpu.get_barrier_semaphore()
    for d in range(1, teams):
        pl.semaphore_signal(
            barrier, inc=1, device_id={"train": away(d)[0], "query": c},
            device_id_type=pl.DeviceIdType.MESH,
        )
    pl.semaphore_signal(
        barrier, inc=1, device_id={"train": t, "query": other},
        device_id_type=pl.DeviceIdType.MESH,
    )
    pl.semaphore_wait(barrier, teams)

    def docs_of(core):
        return pl.ds(pl.multiple_of(core * docs, docs), docs)

    pair = push(own_ref, stacked_ref.at[docs_of(c), :], pair_sem.at[0], pair_sem.at[1], t, other)
    pair.start()
    stacked_ref[docs_of(c), :] = own_ref[...]
    pair.wait()
    turned[:, :half] = stacked_ref[:, pl.ds(pl.multiple_of(c * half, half), half)]
    turned[:, half:] = stacked_ref[:, pl.ds(pl.multiple_of(other * half, half), half)]
    for i in range(half // SIDE):
        lo = i * SIDE
        part[lo : lo + SIDE, :] = dot(
            turned[:, lo : lo + SIDE], turned[:, lo : lo + wide], ((0,), (0,))
        )

    def shares(d):
        to, _ = away(d)
        return push(
            part.at[pl.ds(pl.multiple_of(to * rows, rows), rows), :],
            slots.at[d], sems.at[0, d], sems.at[1, d], to, c,
        )

    for d in range(1, teams):
        shares(d).start()
    total = part[pl.ds(pl.multiple_of(t * rows, rows), rows), :]
    for d in range(1, teams):
        shares(d).wait_recv()
        total = total + slots[d]
    band_ref[mine(t, c), :] = total

    def spreads(d):
        return push(
            band_ref.at[mine(t, c), :], band_ref.at[mine(t, c), :],
            sems.at[2, d], sems.at[3, d], away(d)[0], c,
        )

    def relays(d):
        owner = away(d)[1]
        return push(
            band_ref.at[mine(owner, c), :], band_ref.at[mine(owner, c), :],
            sems.at[4, d], sems.at[5, d], t, other,
        )

    for d in range(1, teams):
        spreads(d).start()
    relays(0).start()
    for d in range(1, teams):
        spreads(d).wait_recv()
        relays(d).start()
    for d in range(teams):
        relays(d).wait_recv()
    for d in range(1, teams):
        shares(d).wait_send()
        spreads(d).wait_send()
    for d in range(teams):
        relays(d).wait_send()


def gram_band(train_grads):
    teams = lax.axis_size("train")
    docs, width = train_grads.shape
    wide = band_width(width)
    rows = width // (2 * teams)
    vmem = pl.BlockSpec(memory_space=pltpu.VMEM)
    return pl.pallas_call(
        functools.partial(gram_kernel, teams),
        out_shape=[
            jax.ShapeDtypeStruct((2 * docs, width), jnp.float32),
            jax.ShapeDtypeStruct((width, wide), jnp.float32),
        ],
        in_specs=[vmem],
        out_specs=[vmem, vmem],
        scratch_shapes=[
            pltpu.VMEM((2 * docs, width), jnp.float32),
            pltpu.VMEM((width // 2, wide), jnp.float32),
            pltpu.VMEM((teams, rows, wide), jnp.float32),
            pltpu.SemaphoreType.DMA((6, teams)),
            pltpu.SemaphoreType.DMA((2,)),
        ],
        compiler_params=pltpu.CompilerParams(
            vmem_limit_bytes=48 * 2**20, collective_id=0, has_side_effects=True
        ),
    )(train_grads)


def factor_kernel(band_ref, a_ref, inv_ref):
    width = band_ref.shape[0]
    count = width // SIDE
    eye = lax.broadcasted_iota(jnp.int32, (SIDE, SIDE), 0) == lax.broadcasted_iota(
        jnp.int32, (SIDE, SIDE), 1
    )
    span = [slice(k * SIDE, (k + 1) * SIDE) for k in range(count)]
    diag = jnp.zeros((SIDE, SIDE), jnp.float32)
    for k in range(count):
        diag = diag + jnp.where(eye, band_ref[span[k], span[0]], 0.0)
    shift = 0.1 * jnp.sum(diag) / width
    for i in range(count):
        for d in range(count // 2 + 1):
            block = band_ref[span[i], span[d]]
            j = (i + d) % count
            if d == 0:
                a_ref[span[i], span[i]] = block + jnp.where(eye, shift, 0.0)
            elif j > i:
                a_ref[span[i], span[j]] = block
            elif 2 * d < count:
                a_ref[span[j], span[i]] = block.T
    for k in range(count):
        inv_ref[k] = a_ref[span[k], span[k]]
        invert_block(inv_ref.at[k])
        if k + 1 == count:
            break
        rest = a_ref[span[k], (k + 1) * SIDE :]
        w = dot(inv_ref[k], rest)
        for i in range(k + 1, count):
            off = (i - k - 1) * SIDE
            a_ref[span[i], i * SIDE :] -= dot(
                rest[:, off : off + SIDE], w[:, off:], ((0,), (0,))
            )
        a_ref[span[k], (k + 1) * SIDE :] = w


def solve_kernel(a_ref, inv_ref, query_ref, out_ref):
    count = inv_ref.shape[0]
    span = [slice(k * SIDE, (k + 1) * SIDE) for k in range(count)]
    out_ref[...] = query_ref[...]
    for k in range(count - 1):
        out_ref[:, (k + 1) * SIDE :] -= dot(
            out_ref[:, span[k]], a_ref[span[k], (k + 1) * SIDE :]
        )
    for k in reversed(range(count)):
        z = dot(out_ref[:, span[k]], inv_ref[k])
        if k + 1 < count:
            z = z - dot(
                out_ref[:, (k + 1) * SIDE :], a_ref[span[k], (k + 1) * SIDE :], ((1,), (1,))
            )
        out_ref[:, span[k]] = z


def factor(band):
    width = band.shape[0]
    vmem = pl.BlockSpec(memory_space=pltpu.VMEM)
    return pl.pallas_call(
        factor_kernel,
        out_shape=[
            jax.ShapeDtypeStruct((width, width), jnp.float32),
            jax.ShapeDtypeStruct((width // SIDE, SIDE, SIDE), jnp.float32),
        ],
        in_specs=[vmem],
        out_specs=[vmem, vmem],
        compiler_params=pltpu.CompilerParams(vmem_limit_bytes=48 * 2**20),
        cost_estimate=pl.CostEstimate(
            flops=12 * width**3, bytes_accessed=256 * 2**20, transcendentals=0
        ),
    )(band)


def solve_rows(upper, inverses, queries):
    vmem = pl.BlockSpec(memory_space=pltpu.VMEM)
    return pl.pallas_call(
        solve_kernel,
        out_shape=jax.ShapeDtypeStruct(queries.shape, jnp.float32),
        in_specs=[vmem, vmem, vmem],
        out_specs=vmem,
        compiler_params=pltpu.CompilerParams(vmem_limit_bytes=48 * 2**20),
    )(upper, inverses, queries)


def shards(train_grads, query_grads):
    width = train_grads.shape[1]
    count_docs = lax.axis_size("train") * lax.axis_size("query") * train_grads.shape[0]
    stacked, band = gram_band(train_grads)
    band, query_grads = lax.optimization_barrier((band, query_grads))
    queries = lax.all_gather(query_grads, "train", axis=1, tiled=True)
    upper, inverses = factor(band)
    precond = solve_rows(upper, inverses, queries)
    scores = jnp.dot(precond, stacked.T, preferred_element_type=jnp.float32, precision=HIGHEST)
    return scores * (count_docs / jnp.sqrt(jnp.float32(width)))


def solution(mesh):
    in_specs = (P(("groups", "train", "query"), None), P(("groups", "query"), "train"))
    out_specs = P(("groups", "query"), "train")
    return jax.shard_map(shards, mesh=mesh, in_specs=in_specs, out_specs=out_specs, check_vma=False)
```

```python
import functools

import jax
import jax.numpy as jnp
from jax import lax
from jax.experimental import pallas as pl
from jax.experimental.pallas import tpu as pltpu
from jax.sharding import PartitionSpec as P

HIGHEST = lax.Precision.HIGHEST
SIDE = 128
ROWS = 8


def dot(a, b, dims=((1,), (0,))):
    return lax.dot_general(
        a, b, (dims, ((), ())), precision=HIGHEST, preferred_element_type=jnp.float32
    )


def invert_small(cols, row):
    for s in range(ROWS):
        inv = 1.0 / jnp.broadcast_to(cols[s][s : s + 1], cols[s].shape)
        here = row == s
        pivot = cols[s]
        out = []
        for j in range(ROWS):
            if j == s:
                out.append(jnp.where(here, inv, -pivot * inv))
            else:
                r = jnp.broadcast_to(cols[j][s : s + 1], pivot.shape) * inv
                out.append(jnp.where(here, r, cols[j] - pivot * r))
        cols = out
    return cols


def spread(block, lane):
    return jnp.take_along_axis(block, jnp.full(block.shape, lane, jnp.int32), axis=1)


def invert_block(d_ref, beside=None):
    panels = SIDE // ROWS
    row = lax.broadcasted_iota(jnp.int32, (ROWS, SIDE), 0)
    lane = lax.broadcasted_iota(jnp.int32, (ROWS, SIDE), 1)

    def panel(g):
        base = g * ROWS
        at = pl.ds(pl.multiple_of(base, ROWS), ROWS)
        own = d_ref[at, :]
        cols = invert_small([spread(own, base + s) for s in range(ROWS)], row)
        inside = (lane >= base) & (lane < base + ROWS)
        start = jnp.where(inside, jnp.where(lane - base == row, 1.0, 0.0), own)
        fresh = cols[0] * jnp.broadcast_to(start[0:1], start.shape)
        for s in range(1, ROWS):
            fresh = fresh + cols[s] * jnp.broadcast_to(start[s : s + 1], start.shape)
        wide = [jnp.broadcast_to(fresh[s : s + 1], fresh.shape) for s in range(ROWS)]
        for i in range(panels):
            block = d_ref[i * ROWS : (i + 1) * ROWS, :]
            new = jnp.where(inside, 0.0, block)
            for s in range(ROWS):
                new = new - spread(block, base + s) * wide[s]
            d_ref[i * ROWS : (i + 1) * ROWS, :] = new
        d_ref[at, :] = fresh

    def step(i, carry):
        if beside is not None:
            beside(i)
        panel(2 * i)
        panel(2 * i + 1)
        return carry

    lax.fori_loop(0, panels // 2, step, 0)


def band_width(width):
    return width // 2 + SIDE


def gram_kernel(teams, own_ref, stacked_ref, band_ref, turned, part, slots, sems, pair_sem):
    docs, width = own_ref.shape
    half, wide = width // 2, band_width(width)
    rows = half // teams
    t, c = lax.axis_index("train"), lax.axis_index("query")
    other = 1 - c

    def mine(team, core):
        return pl.ds(pl.multiple_of(core * half + team * rows, rows), rows)

    def away(d):
        return lax.rem(t + d, teams), lax.rem(t + teams - d, teams)

    def push(src, dst, send, recv, team, core):
        return pltpu.make_async_remote_copy(
            src_ref=src,
            dst_ref=dst,
            send_sem=send,
            recv_sem=recv,
            device_id={"train": team, "query": core},
            device_id_type=pl.DeviceIdType.MESH,
        )

    barrier = pltpu.get_barrier_semaphore()
    for d in range(1, teams):
        pl.semaphore_signal(
            barrier, inc=1, device_id={"train": away(d)[0], "query": c},
            device_id_type=pl.DeviceIdType.MESH,
        )
    pl.semaphore_signal(
        barrier, inc=1, device_id={"train": t, "query": other},
        device_id_type=pl.DeviceIdType.MESH,
    )
    pl.semaphore_wait(barrier, teams)

    def docs_of(core):
        return pl.ds(pl.multiple_of(core * docs, docs), docs)

    pair = push(own_ref, stacked_ref.at[docs_of(c), :], pair_sem.at[0], pair_sem.at[1], t, other)
    pair.start()
    stacked_ref[docs_of(c), :] = own_ref[...]
    pair.wait()
    turned[:, :half] = stacked_ref[:, pl.ds(pl.multiple_of(c * half, half), half)]
    turned[:, half:] = stacked_ref[:, pl.ds(pl.multiple_of(other * half, half), half)]
    def shares(d):
        to, _ = away(d)
        return push(
            part.at[pl.ds(pl.multiple_of(to * rows, rows), rows), :],
            slots.at[d], sems.at[0, d], sems.at[1, d], to, c,
        )

    for i in range(half // SIDE):
        lo = i * SIDE
        part[lo : lo + SIDE, :] = dot(
            turned[:, lo : lo + SIDE], turned[:, lo : lo + wide], ((0,), (0,))
        )
        for to in range(teams):
            if ((to + 1) * rows - 1) // SIDE == i:
                d = lax.rem(to - t + teams, teams)

                @pl.when(d != 0)
                def _():
                    shares(d).start()

    total = part[pl.ds(pl.multiple_of(t * rows, rows), rows), :]
    for d in range(1, teams):
        shares(d).wait_recv()
        total = total + slots[d]
    band_ref[mine(t, c), :] = total

    def spreads(d):
        return push(
            band_ref.at[mine(t, c), :], band_ref.at[mine(t, c), :],
            sems.at[2, d], sems.at[3, d], away(d)[0], c,
        )

    def relays(d):
        owner = away(d)[1]
        return push(
            band_ref.at[mine(owner, c), :], band_ref.at[mine(owner, c), :],
            sems.at[4, d], sems.at[5, d], t, other,
        )

    for d in range(1, teams):
        spreads(d).start()
    relays(0).start()
    for d in range(1, teams):
        spreads(d).wait_recv()
        relays(d).start()
    for d in range(teams):
        relays(d).wait_recv()
    for d in range(1, teams):
        shares(d).wait_send()
        spreads(d).wait_send()
    for d in range(teams):
        relays(d).wait_send()


def gram_band(train_grads):
    teams = lax.axis_size("train")
    docs, width = train_grads.shape
    wide = band_width(width)
    rows = width // (2 * teams)
    vmem = pl.BlockSpec(memory_space=pltpu.VMEM)
    return pl.pallas_call(
        functools.partial(gram_kernel, teams),
        out_shape=[
            jax.ShapeDtypeStruct((2 * docs, width), jnp.float32),
            jax.ShapeDtypeStruct((width, wide), jnp.float32),
        ],
        in_specs=[vmem],
        out_specs=[vmem, vmem],
        scratch_shapes=[
            pltpu.VMEM((2 * docs, width), jnp.float32),
            pltpu.VMEM((width // 2, wide), jnp.float32),
            pltpu.VMEM((teams, rows, wide), jnp.float32),
            pltpu.SemaphoreType.DMA((6, teams)),
            pltpu.SemaphoreType.DMA((2,)),
        ],
        compiler_params=pltpu.CompilerParams(
            vmem_limit_bytes=48 * 2**20, collective_id=0, has_side_effects=True
        ),
    )(train_grads)


def inverse_kernel(band_ref, a_ref, inv_ref, w_ref):
    width = band_ref.shape[0]
    count = width // SIDE
    eye = lax.broadcasted_iota(jnp.int32, (SIDE, SIDE), 0) == lax.broadcasted_iota(
        jnp.int32, (SIDE, SIDE), 1
    )
    span = [slice(k * SIDE, (k + 1) * SIDE) for k in range(count)]
    diag = jnp.zeros((SIDE, SIDE), jnp.float32)
    for k in range(count):
        diag = diag + jnp.where(eye, band_ref[span[k], span[0]], 0.0)
    shift = 0.1 * jnp.sum(diag) / width
    for i in range(count):
        for d in range(count // 2 + 1):
            block = band_ref[span[i], span[d]]
            j = (i + d) % count
            if d == 0:
                block = block + jnp.where(eye, shift, 0.0)
            a_ref[span[i], span[j]] = block
            if 0 < d and 2 * d < count:
                a_ref[span[j], span[i]] = block.T

    def update(k, slot, i):
        at = pl.ds(pl.multiple_of(i * SIDE, SIDE), SIDE)
        old = a_ref[at, :]
        change = dot(old[:, span[k]], w_ref[slot])
        a_ref[at, :] = old - change
        a_ref[at, span[k]] = -change[:, span[k]]

    inv_ref[...] = a_ref[span[0], span[0]]
    invert_block(inv_ref)
    for k in range(count):
        slot = k % 2
        w_ref[slot] = dot(inv_ref[...], a_ref[span[k], :])
        w_ref[slot, :, span[k]] = inv_ref[...]
        work = functools.partial(update, k, slot)
        if k + 1 < count:
            after = span[k + 1]
            inv_ref[...] = a_ref[after, after] - dot(a_ref[after, span[k]], w_ref[slot, :, after])
            steps = SIDE // (2 * ROWS)
            each = -(-count // steps)
            if each * steps == count:
                invert_block(inv_ref, lambda i: [work(i * each + e) for e in range(each)])
            else:
                invert_block(inv_ref)
                lax.fori_loop(0, count, lambda i, c: (work(i), c)[1], 0)
        else:
            lax.fori_loop(0, count, lambda i, c: (work(i), c)[1], 0)
        a_ref[span[k], :] = w_ref[slot]


def damped_inverse(band):
    width = band.shape[0]
    vmem = pl.BlockSpec(memory_space=pltpu.VMEM)
    return pl.pallas_call(
        inverse_kernel,
        out_shape=jax.ShapeDtypeStruct((width, width), jnp.float32),
        in_specs=[vmem],
        out_specs=vmem,
        scratch_shapes=[
            pltpu.VMEM((SIDE, SIDE), jnp.float32),
            pltpu.VMEM((2, SIDE, width), jnp.float32),
        ],
        compiler_params=pltpu.CompilerParams(vmem_limit_bytes=48 * 2**20),
        cost_estimate=pl.CostEstimate(
            flops=12 * width**3, bytes_accessed=256 * 2**20, transcendentals=0
        ),
    )(band)


def shards(train_grads, query_grads):
    width = train_grads.shape[1]
    count_docs = lax.axis_size("train") * lax.axis_size("query") * train_grads.shape[0]
    stacked, band = gram_band(train_grads)
    band, query_grads = lax.optimization_barrier((band, query_grads))
    queries = lax.all_gather(query_grads, "train", axis=1, tiled=True)
    inverse = damped_inverse(band)
    precond = jnp.dot(queries, inverse, preferred_element_type=jnp.float32, precision=HIGHEST)
    scores = jnp.dot(precond, stacked.T, preferred_element_type=jnp.float32, precision=HIGHEST)
    return scores * (count_docs / jnp.sqrt(jnp.float32(width)))


def solution(mesh):
    in_specs = (P(("groups", "train", "query"), None), P(("groups", "query"), "train"))
    out_specs = P(("groups", "query"), "train")
    return jax.shard_map(shards, mesh=mesh, in_specs=in_specs, out_specs=out_specs, check_vma=False)
```

```python
import functools

import jax
import jax.numpy as jnp
from jax import lax
from jax.experimental import pallas as pl
from jax.experimental.pallas import tpu as pltpu
from jax.sharding import PartitionSpec as P

HIGHEST = lax.Precision.HIGHEST
SIDE = 128
ROWS = 8


def dot(a, b, dims=((1,), (0,))):
    return lax.dot_general(
        a, b, (dims, ((), ())), precision=HIGHEST, preferred_element_type=jnp.float32
    )


def parts_of(x):
    high = x.astype(jnp.bfloat16)
    left = x - high.astype(jnp.float32)
    mid = left.astype(jnp.bfloat16)
    return high, mid, (left - mid.astype(jnp.float32)).astype(jnp.bfloat16)


def left_parts(x):
    high, mid, low = parts_of(x)
    return jnp.concatenate([high, high, high, mid, mid, low], axis=1)


def right_parts(x):
    high, mid, low = parts_of(x)
    return jnp.concatenate([high, mid, low, high, mid, high], axis=0)


def tree(terms):
    while len(terms) > 1:
        terms = [a + b for a, b in zip(terms[::2], terms[1::2])]
    return terms[0]


def reciprocal(x):
    r = pl.reciprocal(x, approx=True)
    r = r * (2.0 - x * r)
    return r * (2.0 - x * r)


def invert_small(cols, row):
    for s in range(ROWS):
        inv = reciprocal(jnp.broadcast_to(cols[s][s : s + 1], cols[s].shape))
        here = row == s
        scaled = cols[s] * inv
        out = []
        for j in range(ROWS):
            if j == s:
                out.append(jnp.where(here, inv, -scaled))
            else:
                r = jnp.broadcast_to(cols[j][s : s + 1], scaled.shape)
                out.append(jnp.where(here, r * inv, cols[j] - scaled * r))
        cols = out
    return cols


def spread(block, lane):
    return jnp.take_along_axis(block, jnp.full(block.shape, lane, jnp.int32), axis=1)


def invert_block(d_ref, beside):
    panels = SIDE // ROWS
    row = lax.broadcasted_iota(jnp.int32, (ROWS, SIDE), 0)
    lane = lax.broadcasted_iota(jnp.int32, (ROWS, SIDE), 1)
    for g in range(panels):
        beside(g)
        base = g * ROWS
        blocks = [d_ref[i * ROWS : (i + 1) * ROWS, :] for i in range(panels)]
        own = blocks[g]
        cols = invert_small([spread(own, base + s) for s in range(ROWS)], row)
        inside = (lane >= base) & (lane < base + ROWS)
        start = jnp.where(inside, jnp.where(lane - base == row, 1.0, 0.0), own)
        fresh = tree([cols[s] * jnp.broadcast_to(start[s : s + 1], own.shape) for s in range(ROWS)])
        wide = [jnp.broadcast_to(fresh[s : s + 1], own.shape) for s in range(ROWS)]
        for i in range(panels):
            if i == g:
                new = fresh
            else:
                new = jnp.where(inside, 0.0, blocks[i]) - tree(
                    [spread(blocks[i], base + s) * wide[s] for s in range(ROWS)]
                )
            d_ref[i * ROWS : (i + 1) * ROWS, :] = new


def band_width(width):
    return width // 2 + SIDE


def gram_kernel(teams, own_ref, stacked_ref, band_ref, turned, part, slots, sems, pair_sem):
    docs, width = own_ref.shape
    half, wide = width // 2, band_width(width)
    rows = half // teams
    t, c = lax.axis_index("train"), lax.axis_index("query")
    other = 1 - c

    def mine(team, core):
        return pl.ds(pl.multiple_of(core * half + team * rows, rows), rows)

    def away(d):
        return lax.rem(t + d, teams), lax.rem(t + teams - d, teams)

    def push(src, dst, send, recv, team, core):
        return pltpu.make_async_remote_copy(
            src_ref=src,
            dst_ref=dst,
            send_sem=send,
            recv_sem=recv,
            device_id={"train": team, "query": core},
            device_id_type=pl.DeviceIdType.MESH,
        )

    barrier = pltpu.get_barrier_semaphore()
    for d in range(1, teams):
        pl.semaphore_signal(
            barrier, inc=1, device_id={"train": away(d)[0], "query": c},
            device_id_type=pl.DeviceIdType.MESH,
        )
    pl.semaphore_signal(
        barrier, inc=1, device_id={"train": t, "query": other},
        device_id_type=pl.DeviceIdType.MESH,
    )
    pl.semaphore_wait(barrier, teams)

    def docs_of(core):
        return pl.ds(pl.multiple_of(core * docs, docs), docs)

    pair = push(own_ref, stacked_ref.at[docs_of(c), :], pair_sem.at[0], pair_sem.at[1], t, other)
    pair.start()
    stacked_ref[docs_of(c), :] = own_ref[...]
    pair.wait()
    turned[:, :half] = stacked_ref[:, pl.ds(pl.multiple_of(c * half, half), half)]
    turned[:, half:] = stacked_ref[:, pl.ds(pl.multiple_of(other * half, half), half)]
    def shares(d):
        to, _ = away(d)
        return push(
            part.at[pl.ds(pl.multiple_of(to * rows, rows), rows), :],
            slots.at[d], sems.at[0, d], sems.at[1, d], to, c,
        )

    for i in range(half // SIDE):
        lo = i * SIDE
        part[lo : lo + SIDE, :] = dot(
            turned[:, lo : lo + SIDE], turned[:, lo : lo + wide], ((0,), (0,))
        )
        for to in range(teams):
            if ((to + 1) * rows - 1) // SIDE == i:
                d = lax.rem(to - t + teams, teams)

                @pl.when(d != 0)
                def _():
                    shares(d).start()

    total = part[pl.ds(pl.multiple_of(t * rows, rows), rows), :]
    for d in range(1, teams):
        shares(d).wait_recv()
        total = total + slots[d]
    band_ref[mine(t, c), :] = total

    def spreads(d):
        return push(
            band_ref.at[mine(t, c), :], band_ref.at[mine(t, c), :],
            sems.at[2, d], sems.at[3, d], away(d)[0], c,
        )

    def relays(d):
        owner = away(d)[1]
        return push(
            band_ref.at[mine(owner, c), :], band_ref.at[mine(owner, c), :],
            sems.at[4, d], sems.at[5, d], t, other,
        )

    for d in range(1, teams):
        spreads(d).start()
    relays(0).start()
    for d in range(1, teams):
        spreads(d).wait_recv()
        relays(d).start()
    for d in range(teams):
        relays(d).wait_recv()
    for d in range(1, teams):
        shares(d).wait_send()
        spreads(d).wait_send()
    for d in range(teams):
        relays(d).wait_send()


def gram_band(train_grads):
    teams = lax.axis_size("train")
    docs, width = train_grads.shape
    wide = band_width(width)
    rows = width // (2 * teams)
    vmem = pl.BlockSpec(memory_space=pltpu.VMEM)
    return pl.pallas_call(
        functools.partial(gram_kernel, teams),
        out_shape=[
            jax.ShapeDtypeStruct((2 * docs, width), jnp.float32),
            jax.ShapeDtypeStruct((width, wide), jnp.float32),
        ],
        in_specs=[vmem],
        out_specs=[vmem, vmem],
        scratch_shapes=[
            pltpu.VMEM((2 * docs, width), jnp.float32),
            pltpu.VMEM((width // 2, wide), jnp.float32),
            pltpu.VMEM((teams, rows, wide), jnp.float32),
            pltpu.SemaphoreType.DMA((6, teams)),
            pltpu.SemaphoreType.DMA((2,)),
        ],
        compiler_params=pltpu.CompilerParams(
            vmem_limit_bytes=48 * 2**20, collective_id=0, has_side_effects=True
        ),
    )(train_grads)


def inverse_kernel(band_ref, a_ref, inv_ref, w_ref, terms_ref):
    width = band_ref.shape[0]
    count = width // SIDE
    eye = lax.broadcasted_iota(jnp.int32, (SIDE, SIDE), 0) == lax.broadcasted_iota(
        jnp.int32, (SIDE, SIDE), 1
    )
    span = [slice(k * SIDE, (k + 1) * SIDE) for k in range(count)]
    diag = jnp.zeros((SIDE, SIDE), jnp.float32)
    for k in range(count):
        diag = diag + jnp.where(eye, band_ref[span[k], span[0]], 0.0)
    shift = 0.1 * jnp.sum(diag) / width
    for i in range(count):
        for d in range(count // 2 + 1):
            block = band_ref[span[i], span[d]]
            j = (i + d) % count
            if d == 0:
                block = block + jnp.where(eye, shift, 0.0)
            a_ref[span[i], span[j]] = block
            if 0 < d and 2 * d < count:
                a_ref[span[j], span[i]] = block.T

    def cut(k):
        return pl.ds(pl.multiple_of(k * SIDE, SIDE), SIDE)

    def update(i, k, ready):
        rows, cols = cut(i), cut(k)
        own = a_ref[rows, cols]
        change = jnp.dot(left_parts(own), terms_ref[...], preferred_element_type=jnp.float32)
        a_ref[rows, :] = a_ref[rows, :] - change
        there = jnp.dot(
            left_parts(own), terms_ref[:, cols], preferred_element_type=jnp.float32
        )
        a_ref[rows, cols] = jnp.where(ready, -there, own)

    w_ref[...] = jnp.zeros_like(w_ref)
    terms_ref[...] = jnp.zeros_like(terms_ref)
    inv_ref[...] = a_ref[span[0], span[0]]
    panels = SIDE // ROWS

    def step(k, carry):
        last = jnp.maximum(k - 1, 0)

        def beside(g):
            for i in range(g * count // panels, (g + 1) * count // panels):
                update(i, last, k > 0)

        invert_block(inv_ref, beside)

        @pl.when(k > 0)
        def _():
            a_ref[cut(last), :] = w_ref[...]

        inverse = inv_ref[...]
        w_ref[...] = jnp.dot(
            left_parts(inverse), right_parts(a_ref[cut(k), :]), preferred_element_type=jnp.float32
        )
        w_ref[:, cut(k)] = inverse
        terms_ref[...] = right_parts(w_ref[...])
        after = cut(jnp.minimum(k + 1, count - 1))
        inv_ref[...] = a_ref[after, after] - jnp.dot(
            left_parts(a_ref[after, cut(k)]),
            terms_ref[:, after],
            preferred_element_type=jnp.float32,
        )
        return carry

    lax.fori_loop(0, count, step, 0)
    for i in range(count - 1):
        update(i, count - 1, True)
    a_ref[span[count - 1], :] = w_ref[...]


def damped_inverse(band):
    width = band.shape[0]
    vmem = pl.BlockSpec(memory_space=pltpu.VMEM)
    return pl.pallas_call(
        inverse_kernel,
        out_shape=jax.ShapeDtypeStruct((width, width), jnp.float32),
        in_specs=[vmem],
        out_specs=vmem,
        scratch_shapes=[
            pltpu.VMEM((SIDE, SIDE), jnp.float32),
            pltpu.VMEM((SIDE, width), jnp.float32),
            pltpu.VMEM((6 * SIDE, width), jnp.bfloat16),
        ],
        compiler_params=pltpu.CompilerParams(vmem_limit_bytes=48 * 2**20),
        cost_estimate=pl.CostEstimate(
            flops=12 * width**3, bytes_accessed=256 * 2**20, transcendentals=0
        ),
    )(band)


def shards(train_grads, query_grads):
    width = train_grads.shape[1]
    count_docs = lax.axis_size("train") * lax.axis_size("query") * train_grads.shape[0]
    stacked, band = gram_band(train_grads)
    band, query_grads = lax.optimization_barrier((band, query_grads))
    queries = lax.all_gather(query_grads, "train", axis=1, tiled=True)
    inverse = damped_inverse(band)
    precond = jnp.dot(queries, inverse, preferred_element_type=jnp.float32, precision=HIGHEST)
    scores = jnp.dot(precond, stacked.T, preferred_element_type=jnp.float32, precision=HIGHEST)
    return scores * (count_docs / jnp.sqrt(jnp.float32(width)))


def solution(mesh):
    in_specs = (P(("groups", "train", "query"), None), P(("groups", "query"), "train"))
    out_specs = P(("groups", "query"), "train")
    return jax.shard_map(shards, mesh=mesh, in_specs=in_specs, out_specs=out_specs, check_vma=False)
```

```python
import functools

import jax
import jax.numpy as jnp
from jax import lax
from jax.experimental import pallas as pl
from jax.experimental.pallas import tpu as pltpu
from jax.sharding import PartitionSpec as P

HIGHEST = lax.Precision.HIGHEST
SIDE = 128
ROWS = 8


def dot(a, b, dims=((1,), (0,))):
    return lax.dot_general(
        a, b, (dims, ((), ())), precision=HIGHEST, preferred_element_type=jnp.float32
    )


def parts_of(x):
    high = x.astype(jnp.bfloat16)
    left = x - high.astype(jnp.float32)
    mid = left.astype(jnp.bfloat16)
    return high, mid, (left - mid.astype(jnp.float32)).astype(jnp.bfloat16)


def left_parts(x):
    high, mid, low = parts_of(x)
    return jnp.concatenate([high, high, high, mid, mid, low], axis=1)


def right_parts(x):
    high, mid, low = parts_of(x)
    return jnp.concatenate([high, mid, low, high, mid, high], axis=0)


def tree(terms):
    while len(terms) > 1:
        terms = [a + b for a, b in zip(terms[::2], terms[1::2])]
    return terms[0]


def reciprocal(x):
    r = pl.reciprocal(x, approx=True)
    r = r * (2.0 - x * r)
    return r * (2.0 - x * r)


def invert_small(cols, row):
    for s in range(ROWS):
        inv = reciprocal(jnp.broadcast_to(cols[s][s : s + 1], cols[s].shape))
        here = row == s
        scaled = cols[s] * inv
        out = []
        for j in range(ROWS):
            if j == s:
                out.append(jnp.where(here, inv, -scaled))
            else:
                r = jnp.broadcast_to(cols[j][s : s + 1], scaled.shape)
                out.append(jnp.where(here, r * inv, cols[j] - scaled * r))
        cols = out
    return cols


def spread(block, lane):
    return jnp.take_along_axis(block, jnp.full(block.shape, lane, jnp.int32), axis=1)


def invert_block(d_ref, beside):
    panels = SIDE // ROWS
    row = lax.broadcasted_iota(jnp.int32, (ROWS, SIDE), 0)
    lane = lax.broadcasted_iota(jnp.int32, (ROWS, SIDE), 1)
    for g in range(panels):
        beside(g)
        base = g * ROWS
        blocks = [d_ref[i * ROWS : (i + 1) * ROWS, :] for i in range(panels)]
        own = blocks[g]
        cols = invert_small([spread(own, base + s) for s in range(ROWS)], row)
        inside = (lane >= base) & (lane < base + ROWS)
        start = jnp.where(inside, jnp.where(lane - base == row, 1.0, 0.0), own)
        fresh = tree([cols[s] * jnp.broadcast_to(start[s : s + 1], own.shape) for s in range(ROWS)])
        wide = [jnp.broadcast_to(fresh[s : s + 1], own.shape) for s in range(ROWS)]
        for i in range(panels):
            if i == g:
                new = fresh
            else:
                new = jnp.where(inside, 0.0, blocks[i]) - tree(
                    [spread(blocks[i], base + s) * wide[s] for s in range(ROWS)]
                )
            d_ref[i * ROWS : (i + 1) * ROWS, :] = new


def band_width(width):
    return width // 2 + SIDE


def gram_kernel(teams, own_ref, stacked_ref, band_ref, turned, part, near, far, sems, core_sems, pair_sem):
    docs, width = own_ref.shape
    half, wide = width // 2, band_width(width)
    rows = half // teams
    pairs = teams // 2
    t, c = lax.axis_index("train"), lax.axis_index("query")
    other = 1 - c
    u, y = t // 2, t % 2
    mate = t + 1 - 2 * y

    def ahead(d):
        return (u + d) % pairs

    def behind(d):
        return (u + pairs - d) % pairs

    def mine(team):
        return pl.ds(pl.multiple_of(c * half + team * rows, rows), rows)

    def share(team):
        return pl.ds(pl.multiple_of(team * rows, rows), rows)

    def push(src, dst, send, recv, team, core):
        return pltpu.make_async_remote_copy(
            src_ref=src,
            dst_ref=dst,
            send_sem=send,
            recv_sem=recv,
            device_id={"train": team, "query": core},
            device_id_type=pl.DeviceIdType.MESH,
        )

    barrier = pltpu.get_barrier_semaphore()
    for team, core in [(2 * ahead(d) + y, c) for d in range(1, pairs)] + [(mate, c), (t, other)]:
        pl.semaphore_signal(
            barrier, inc=1, device_id={"train": team, "query": core},
            device_id_type=pl.DeviceIdType.MESH,
        )
    pl.semaphore_wait(barrier, pairs + 1)

    def docs_of(core):
        return pl.ds(pl.multiple_of(core * docs, docs), docs)

    pair = push(own_ref, stacked_ref.at[docs_of(c), :], pair_sem.at[0], pair_sem.at[1], t, other)
    pair.start()
    stacked_ref[docs_of(c), :] = own_ref[...]
    pair.wait()
    turned[:, :half] = stacked_ref[:, pl.ds(pl.multiple_of(c * half, half), half)]
    turned[:, half:] = stacked_ref[:, pl.ds(pl.multiple_of(other * half, half), half)]

    def to_mate(v):
        return push(
            part.at[share(2 * v + 1 - y), :], near.at[v], sems.at[0, v], sems.at[1, v], mate, c
        )

    def to_owner(d):
        team = 2 * ahead(d) + y
        return push(
            part.at[share(team), :], far.at[d], sems.at[2, d], sems.at[3, d], team, c
        )

    for i in range(half // SIDE):
        lo = i * SIDE
        part[lo : lo + SIDE, :] = dot(
            turned[:, lo : lo + SIDE], turned[:, lo : lo + wide], ((0,), (0,))
        )
        for v in range(pairs):
            if ((2 * v + 2) * rows - 1) // SIDE == i:
                to_mate(v).start()
    for d in range(1, pairs):
        v = ahead(d)
        to_mate(v).wait_recv()
        part[share(2 * v + y), :] = part[share(2 * v + y), :] + near[v]
        to_owner(d).start()
    to_mate(u).wait_recv()
    total = part[share(t), :] + near[u]
    for d in range(1, pairs):
        to_owner(d).wait_recv()
        total = total + far[d]
    band_ref[mine(t), :] = total

    def spread_far(d):
        piece = band_ref.at[mine(t), :]
        return push(piece, piece, sems.at[4, d], sems.at[5, d], 2 * ahead(d) + y, c)

    def spread_near(d):
        piece = band_ref.at[mine(2 * behind(d) + y), :]
        return push(piece, piece, sems.at[6, d], sems.at[7, d], mate, c)

    def spread_core(d, q):
        piece = band_ref.at[mine(2 * behind(d) + (y if q == 0 else 1 - y)), :]
        return push(
            piece, piece, core_sems.at[0, 2 * d + q], core_sems.at[1, 2 * d + q], t, other
        )

    for d in range(1, pairs):
        spread_far(d).start()
    spread_near(0).start()
    spread_core(0, 0).start()
    for d in range(1, pairs):
        spread_far(d).wait_recv()
        spread_near(d).start()
        spread_core(d, 0).start()
    for d in range(pairs):
        spread_near(d).wait_recv()
        spread_core(d, 1).start()
    for d in range(pairs):
        spread_core(d, 0).wait_recv()
        spread_core(d, 1).wait_recv()
    for d in range(pairs):
        to_mate(d).wait_send()
        spread_near(d).wait_send()
        spread_core(d, 0).wait_send()
        spread_core(d, 1).wait_send()
        if d:
            to_owner(d).wait_send()
            spread_far(d).wait_send()


def gram_band(train_grads):
    teams = lax.axis_size("train")
    docs, width = train_grads.shape
    wide = band_width(width)
    rows = width // (2 * teams)
    vmem = pl.BlockSpec(memory_space=pltpu.VMEM)
    return pl.pallas_call(
        functools.partial(gram_kernel, teams),
        out_shape=[
            jax.ShapeDtypeStruct((2 * docs, width), jnp.float32),
            jax.ShapeDtypeStruct((width, wide), jnp.float32),
        ],
        in_specs=[vmem],
        out_specs=[vmem, vmem],
        scratch_shapes=[
            pltpu.VMEM((2 * docs, width), jnp.float32),
            pltpu.VMEM((width // 2, wide), jnp.float32),
            pltpu.VMEM((teams // 2, rows, wide), jnp.float32),
            pltpu.VMEM((teams // 2, rows, wide), jnp.float32),
            pltpu.SemaphoreType.DMA((8, teams // 2)),
            pltpu.SemaphoreType.DMA((2, teams)),
            pltpu.SemaphoreType.DMA((2,)),
        ],
        compiler_params=pltpu.CompilerParams(
            vmem_limit_bytes=48 * 2**20, collective_id=0, has_side_effects=True
        ),
    )(train_grads)


def inverse_kernel(band_ref, a_ref, inv_ref, w_ref, terms_ref):
    width = band_ref.shape[0]
    count = width // SIDE
    eye = lax.broadcasted_iota(jnp.int32, (SIDE, SIDE), 0) == lax.broadcasted_iota(
        jnp.int32, (SIDE, SIDE), 1
    )
    span = [slice(k * SIDE, (k + 1) * SIDE) for k in range(count)]
    diag = jnp.zeros((SIDE, SIDE), jnp.float32)
    for k in range(count):
        diag = diag + jnp.where(eye, band_ref[span[k], span[0]], 0.0)
    shift = 0.1 * jnp.sum(diag) / width
    for i in range(count):
        for d in range(count // 2 + 1):
            block = band_ref[span[i], span[d]]
            j = (i + d) % count
            if d == 0:
                block = block + jnp.where(eye, shift, 0.0)
            a_ref[span[i], span[j]] = block
            if 0 < d and 2 * d < count:
                a_ref[span[j], span[i]] = block.T

    def cut(k):
        return pl.ds(pl.multiple_of(k * SIDE, SIDE), SIDE)

    def update(i, k, ready):
        rows, cols = cut(i), cut(k)
        own = a_ref[rows, cols]
        change = jnp.dot(left_parts(own), terms_ref[...], preferred_element_type=jnp.float32)
        a_ref[rows, :] = a_ref[rows, :] - change
        there = jnp.dot(
            left_parts(own), terms_ref[:, cols], preferred_element_type=jnp.float32
        )
        a_ref[rows, cols] = jnp.where(ready, -there, own)

    w_ref[...] = jnp.zeros_like(w_ref)
    terms_ref[...] = jnp.zeros_like(terms_ref)
    inv_ref[...] = a_ref[span[0], span[0]]
    panels = SIDE // ROWS

    def step(k, carry):
        last = jnp.maximum(k - 1, 0)

        def beside(g):
            for i in range(g * count // panels, (g + 1) * count // panels):
                update(i, last, k > 0)

        invert_block(inv_ref, beside)

        @pl.when(k > 0)
        def _():
            a_ref[cut(last), :] = w_ref[...]

        inverse = inv_ref[...]
        w_ref[...] = jnp.dot(
            left_parts(inverse), right_parts(a_ref[cut(k), :]), preferred_element_type=jnp.float32
        )
        w_ref[:, cut(k)] = inverse
        terms_ref[...] = right_parts(w_ref[...])
        after = cut(jnp.minimum(k + 1, count - 1))
        inv_ref[...] = a_ref[after, after] - jnp.dot(
            left_parts(a_ref[after, cut(k)]),
            terms_ref[:, after],
            preferred_element_type=jnp.float32,
        )
        return carry

    lax.fori_loop(0, count, step, 0)
    for i in range(count - 1):
        update(i, count - 1, True)
    a_ref[span[count - 1], :] = w_ref[...]


def damped_inverse(band):
    width = band.shape[0]
    vmem = pl.BlockSpec(memory_space=pltpu.VMEM)
    return pl.pallas_call(
        inverse_kernel,
        out_shape=jax.ShapeDtypeStruct((width, width), jnp.float32),
        in_specs=[vmem],
        out_specs=vmem,
        scratch_shapes=[
            pltpu.VMEM((SIDE, SIDE), jnp.float32),
            pltpu.VMEM((SIDE, width), jnp.float32),
            pltpu.VMEM((6 * SIDE, width), jnp.bfloat16),
        ],
        compiler_params=pltpu.CompilerParams(vmem_limit_bytes=48 * 2**20),
        cost_estimate=pl.CostEstimate(
            flops=12 * width**3, bytes_accessed=256 * 2**20, transcendentals=0
        ),
    )(band)


def shards(train_grads, query_grads):
    width = train_grads.shape[1]
    count_docs = lax.axis_size("train") * lax.axis_size("query") * train_grads.shape[0]
    stacked, band = gram_band(train_grads)
    band, query_grads = lax.optimization_barrier((band, query_grads))
    queries = lax.all_gather(query_grads, "train", axis=1, tiled=True)
    inverse = damped_inverse(band)
    precond = jnp.dot(queries, inverse, preferred_element_type=jnp.float32, precision=HIGHEST)
    scores = jnp.dot(precond, stacked.T, preferred_element_type=jnp.float32, precision=HIGHEST)
    return scores * (count_docs / jnp.sqrt(jnp.float32(width)))


def solution(mesh):
    in_specs = (P(("groups", "train", "query"), None), P(("groups", "query"), "train"))
    out_specs = P(("groups", "query"), "train")
    return jax.shard_map(shards, mesh=mesh, in_specs=in_specs, out_specs=out_specs, check_vma=False)
```

```python
import functools

import jax
import jax.numpy as jnp
from jax import lax
from jax.experimental import pallas as pl
from jax.experimental.pallas import tpu as pltpu
from jax.sharding import PartitionSpec as P

HIGHEST = lax.Precision.HIGHEST
SIDE = 128
ROWS = 8


def dot(a, b, dims=((1,), (0,))):
    return lax.dot_general(
        a, b, (dims, ((), ())), precision=HIGHEST, preferred_element_type=jnp.float32
    )


def parts_of(x):
    high = x.astype(jnp.bfloat16)
    left = x - high.astype(jnp.float32)
    mid = left.astype(jnp.bfloat16)
    return high, mid, (left - mid.astype(jnp.float32)).astype(jnp.bfloat16)


def left_parts(x):
    high, mid, low = parts_of(x)
    return jnp.concatenate([high, high, high, mid, mid, low], axis=1)


def right_parts(x):
    high, mid, low = parts_of(x)
    return jnp.concatenate([high, mid, low, high, mid, high], axis=0)


def tree(terms):
    while len(terms) > 1:
        terms = [a + b for a, b in zip(terms[::2], terms[1::2])]
    return terms[0]


def reciprocal(x):
    r = pl.reciprocal(x, approx=True)
    r = r * (2.0 - x * r)
    return r * (2.0 - x * r)


def invert_small(cols, row):
    for s in range(ROWS):
        inv = reciprocal(jnp.broadcast_to(cols[s][s : s + 1], cols[s].shape))
        here = row == s
        scaled = cols[s] * inv
        out = []
        for j in range(ROWS):
            if j == s:
                out.append(jnp.where(here, inv, -scaled))
            else:
                r = jnp.broadcast_to(cols[j][s : s + 1], scaled.shape)
                out.append(jnp.where(here, r * inv, cols[j] - scaled * r))
        cols = out
    return cols


def spread(block, lane):
    return jnp.take_along_axis(block, jnp.full(block.shape, lane, jnp.int32), axis=1)


def invert_block(d_ref, beside):
    panels = SIDE // ROWS
    row = lax.broadcasted_iota(jnp.int32, (ROWS, SIDE), 0)
    lane = lax.broadcasted_iota(jnp.int32, (ROWS, SIDE), 1)
    for g in range(panels):
        beside(g)
        base = g * ROWS
        blocks = [d_ref[i * ROWS : (i + 1) * ROWS, :] for i in range(panels)]
        own = blocks[g]
        cols = invert_small([spread(own, base + s) for s in range(ROWS)], row)
        inside = (lane >= base) & (lane < base + ROWS)
        start = jnp.where(inside, jnp.where(lane - base == row, 1.0, 0.0), own)
        fresh = tree([cols[s] * jnp.broadcast_to(start[s : s + 1], own.shape) for s in range(ROWS)])
        wide = [jnp.broadcast_to(fresh[s : s + 1], own.shape) for s in range(ROWS)]
        for i in range(panels):
            if i == g:
                new = fresh
            else:
                new = jnp.where(inside, 0.0, blocks[i]) - tree(
                    [spread(blocks[i], base + s) * wide[s] for s in range(ROWS)]
                )
            d_ref[i * ROWS : (i + 1) * ROWS, :] = new


def band_width(width):
    return width // 2 + SIDE


def gram_kernel(teams, own_ref, stacked_ref, band_ref, turned, part, near, far, sems, core_sems, pair_sem):
    docs, width = own_ref.shape
    half, wide = width // 2, band_width(width)
    rows = half // teams
    pairs = teams // 2
    t, c = lax.axis_index("train"), lax.axis_index("query")
    other = 1 - c
    u, y = t // 2, t % 2
    mate = t + 1 - 2 * y

    def ahead(d):
        return (u + d) % pairs

    def behind(d):
        return (u + pairs - d) % pairs

    def mine(team):
        return pl.ds(pl.multiple_of(c * half + team * rows, rows), rows)

    def share(team):
        return pl.ds(pl.multiple_of(team * rows, rows), rows)

    def push(src, dst, send, recv, team, core):
        return pltpu.make_async_remote_copy(
            src_ref=src,
            dst_ref=dst,
            send_sem=send,
            recv_sem=recv,
            device_id={"train": team, "query": core},
            device_id_type=pl.DeviceIdType.MESH,
        )

    barrier = pltpu.get_barrier_semaphore()
    for team, core in [(2 * ahead(d) + y, c) for d in range(1, pairs)] + [(mate, c), (t, other)]:
        pl.semaphore_signal(
            barrier, inc=1, device_id={"train": team, "query": core},
            device_id_type=pl.DeviceIdType.MESH,
        )
    pl.semaphore_wait(barrier, pairs + 1)

    def docs_of(core):
        return pl.ds(pl.multiple_of(core * docs, docs), docs)

    pair = push(own_ref, stacked_ref.at[docs_of(c), :], pair_sem.at[0], pair_sem.at[1], t, other)
    pair.start()
    stacked_ref[docs_of(c), :] = own_ref[...]

    def turn(core):
        at = docs_of(core)
        turned[at, :half] = stacked_ref[at, pl.ds(pl.multiple_of(c * half, half), half)]
        turned[at, half:] = stacked_ref[at, pl.ds(pl.multiple_of(other * half, half), half)]

    def product(core, lo):
        at = docs_of(core)
        return dot(turned[at, lo : lo + SIDE], turned[at, lo : lo + wide], ((0,), (0,)))

    turn(c)
    for i in range(half // SIDE):
        part[i * SIDE : (i + 1) * SIDE, :] = product(c, i * SIDE)
    pair.wait()
    turn(other)

    def to_mate(v):
        return push(
            part.at[share(2 * v + 1 - y), :], near.at[v], sems.at[0, v], sems.at[1, v], mate, c
        )

    def to_owner(d):
        team = 2 * ahead(d) + y
        return push(
            part.at[share(team), :], far.at[d], sems.at[2, d], sems.at[3, d], team, c
        )

    for i in range(half // SIDE):
        lo = i * SIDE
        part[lo : lo + SIDE, :] += product(other, lo)
        for v in range(pairs):
            if ((2 * v + 2) * rows - 1) // SIDE == i:
                to_mate(v).start()
    for d in range(1, pairs):
        v = ahead(d)
        to_mate(v).wait_recv()
        part[share(2 * v + y), :] = part[share(2 * v + y), :] + near[v]
        to_owner(d).start()
    to_mate(u).wait_recv()
    total = part[share(t), :] + near[u]
    for d in range(1, pairs):
        to_owner(d).wait_recv()
        total = total + far[d]
    band_ref[mine(t), :] = total

    def spread_far(d):
        piece = band_ref.at[mine(t), :]
        return push(piece, piece, sems.at[4, d], sems.at[5, d], 2 * ahead(d) + y, c)

    def spread_near(d):
        piece = band_ref.at[mine(2 * behind(d) + y), :]
        return push(piece, piece, sems.at[6, d], sems.at[7, d], mate, c)

    def spread_core(d, q):
        piece = band_ref.at[mine(2 * behind(d) + (y if q == 0 else 1 - y)), :]
        return push(
            piece, piece, core_sems.at[0, 2 * d + q], core_sems.at[1, 2 * d + q], t, other
        )

    for d in range(1, pairs):
        spread_far(d).start()
    spread_near(0).start()
    spread_core(0, 0).start()
    for d in range(1, pairs):
        spread_far(d).wait_recv()
        spread_near(d).start()
        spread_core(d, 0).start()
    for d in range(pairs):
        spread_near(d).wait_recv()
        spread_core(d, 1).start()
    for d in range(pairs):
        spread_core(d, 0).wait_recv()
        spread_core(d, 1).wait_recv()
    for d in range(pairs):
        to_mate(d).wait_send()
        spread_near(d).wait_send()
        spread_core(d, 0).wait_send()
        spread_core(d, 1).wait_send()
        if d:
            to_owner(d).wait_send()
            spread_far(d).wait_send()


def gram_band(train_grads):
    teams = lax.axis_size("train")
    docs, width = train_grads.shape
    wide = band_width(width)
    rows = width // (2 * teams)
    vmem = pl.BlockSpec(memory_space=pltpu.VMEM)
    return pl.pallas_call(
        functools.partial(gram_kernel, teams),
        out_shape=[
            jax.ShapeDtypeStruct((2 * docs, width), jnp.float32),
            jax.ShapeDtypeStruct((width, wide), jnp.float32),
        ],
        in_specs=[vmem],
        out_specs=[vmem, vmem],
        scratch_shapes=[
            pltpu.VMEM((2 * docs, width), jnp.float32),
            pltpu.VMEM((width // 2, wide), jnp.float32),
            pltpu.VMEM((teams // 2, rows, wide), jnp.float32),
            pltpu.VMEM((teams // 2, rows, wide), jnp.float32),
            pltpu.SemaphoreType.DMA((8, teams // 2)),
            pltpu.SemaphoreType.DMA((2, teams)),
            pltpu.SemaphoreType.DMA((2,)),
        ],
        compiler_params=pltpu.CompilerParams(
            vmem_limit_bytes=48 * 2**20, collective_id=0, has_side_effects=True
        ),
    )(train_grads)


def inverse_kernel(band_ref, a_ref, inv_ref, w_ref, terms_ref):
    width = band_ref.shape[0]
    count = width // SIDE
    eye = lax.broadcasted_iota(jnp.int32, (SIDE, SIDE), 0) == lax.broadcasted_iota(
        jnp.int32, (SIDE, SIDE), 1
    )
    span = [slice(k * SIDE, (k + 1) * SIDE) for k in range(count)]
    diag = jnp.zeros((SIDE, SIDE), jnp.float32)
    for k in range(count):
        diag = diag + jnp.where(eye, band_ref[span[k], span[0]], 0.0)
    shift = 0.1 * jnp.sum(diag) / width
    for i in range(count):
        for d in range(count // 2 + 1):
            block = band_ref[span[i], span[d]]
            j = (i + d) % count
            if d == 0:
                block = block + jnp.where(eye, shift, 0.0)
            a_ref[span[i], span[j]] = block
            if 0 < d and 2 * d < count:
                a_ref[span[j], span[i]] = block.T

    def cut(k):
        return pl.ds(pl.multiple_of(k * SIDE, SIDE), SIDE)

    def update(i, k, ready):
        rows, cols = cut(i), cut(k)
        own = a_ref[rows, cols]
        change = jnp.dot(left_parts(own), terms_ref[...], preferred_element_type=jnp.float32)
        a_ref[rows, :] = a_ref[rows, :] - change
        there = jnp.dot(
            left_parts(own), terms_ref[:, cols], preferred_element_type=jnp.float32
        )
        a_ref[rows, cols] = jnp.where(ready, -there, own)

    w_ref[...] = jnp.zeros_like(w_ref)
    terms_ref[...] = jnp.zeros_like(terms_ref)
    inv_ref[...] = a_ref[span[0], span[0]]
    panels = SIDE // ROWS

    def step(k, carry):
        last = jnp.maximum(k - 1, 0)

        def beside(g):
            for i in range(g * count // panels, (g + 1) * count // panels):
                update(i, last, k > 0)

        invert_block(inv_ref, beside)

        @pl.when(k > 0)
        def _():
            a_ref[cut(last), :] = w_ref[...]

        inverse = inv_ref[...]
        w_ref[...] = jnp.dot(
            left_parts(inverse), right_parts(a_ref[cut(k), :]), preferred_element_type=jnp.float32
        )
        w_ref[:, cut(k)] = inverse
        terms_ref[...] = right_parts(w_ref[...])
        after = cut(jnp.minimum(k + 1, count - 1))
        inv_ref[...] = a_ref[after, after] - jnp.dot(
            left_parts(a_ref[after, cut(k)]),
            terms_ref[:, after],
            preferred_element_type=jnp.float32,
        )
        return carry

    lax.fori_loop(0, count, step, 0)
    for i in range(count - 1):
        update(i, count - 1, True)
    a_ref[span[count - 1], :] = w_ref[...]


def damped_inverse(band):
    width = band.shape[0]
    vmem = pl.BlockSpec(memory_space=pltpu.VMEM)
    return pl.pallas_call(
        inverse_kernel,
        out_shape=jax.ShapeDtypeStruct((width, width), jnp.float32),
        in_specs=[vmem],
        out_specs=vmem,
        scratch_shapes=[
            pltpu.VMEM((SIDE, SIDE), jnp.float32),
            pltpu.VMEM((SIDE, width), jnp.float32),
            pltpu.VMEM((6 * SIDE, width), jnp.bfloat16),
        ],
        compiler_params=pltpu.CompilerParams(vmem_limit_bytes=48 * 2**20),
        cost_estimate=pl.CostEstimate(
            flops=12 * width**3, bytes_accessed=256 * 2**20, transcendentals=0
        ),
    )(band)


def shards(train_grads, query_grads):
    width = train_grads.shape[1]
    count_docs = lax.axis_size("train") * lax.axis_size("query") * train_grads.shape[0]
    stacked, band = gram_band(train_grads)
    band, query_grads = lax.optimization_barrier((band, query_grads))
    queries = lax.all_gather(query_grads, "train", axis=1, tiled=True)
    inverse = damped_inverse(band)
    precond = jnp.dot(queries, inverse, preferred_element_type=jnp.float32, precision=HIGHEST)
    scores = jnp.dot(precond, stacked.T, preferred_element_type=jnp.float32, precision=HIGHEST)
    return scores * (count_docs / jnp.sqrt(jnp.float32(width)))


def solution(mesh):
    in_specs = (P(("groups", "train", "query"), None), P(("groups", "query"), "train"))
    out_specs = P(("groups", "query"), "train")
    return jax.shard_map(shards, mesh=mesh, in_specs=in_specs, out_specs=out_specs, check_vma=False)
```
